32 devices in a mesh: groups: 2 (over y), seq: 4 (over z), chan: 4 (over x, core).
Axes of the slice: x: 2, y: 2, z: 4, core: 2. Of those that a mesh axis runs over, the one named last changes fastest.
Arguments:
- query: bfloat16 [16384, 1024], P(('groups', 'seq'), 'chan'), parts along dimension 0, may hold values from -6 to 6
- keyed: bfloat16 [16384, 1024], P(('groups', 'seq'), 'chan'), parts along dimension 0, may hold values from -6 to 6
- values: bfloat16 [16384, 1024], P(('groups', 'seq'), 'chan'), parts along dimension 0, may hold values from -6 to 6
- cotangent: bfloat16 [16384, 1024], P(('groups', 'seq'), 'chan'), parts along dimension 0, may hold values from -6 to 6
- segment_ids: int32 [16384], P(('groups', 'seq')), parts along dimension 0, may hold values from 0 to 7, never falling along the last dimension, each value on 1 to 2048 neighbouring positions
- positions: bfloat16 [16384, 64], P(('groups', 'seq')), parts along dimension 0, may hold values from -6 to 6
- filter_weight: bfloat16 [64, 1024], P('seq', 'chan'), may hold values from -0.75 to 0.75
- skip_gain: float32 [1024], P('chan'), may hold values from 0.5 to 1.5
- first_factor: bfloat16 [256, 256], replicated, may hold values from -0.375 to 0.375
- second_factor: bfloat16 [8, 8], replicated, may hold values from -2 to 2
- self_coef: bfloat16 [2, 4, 2048], P(None, 'seq'), may hold values from -4 to 4
- cross_coef: bfloat16 [2, 4, 2048], P(None, 'seq'), may hold values from -4 to 4
Outputs:
- mixed: bfloat16 [16384, 1024], P(('groups', 'seq'), 'chan'), parts along dimension 0
- grad_query: bfloat16 [16384, 1024], P(('groups', 'seq'), 'chan'), parts along dimension 0
- grad_keyed: bfloat16 [16384, 1024], P(('groups', 'seq'), 'chan'), parts along dimension 0
- grad_values: bfloat16 [16384, 1024], P(('groups', 'seq'), 'chan'), parts along dimension 0
- grad_filter: float32 [128, 1024], P(('groups', 'seq'), 'chan'), parts along dimension 0
The draws below stay inside these ranges and needn't reach their ends.
There are 2 independent parts, one for each index of `groups`. The reference program is written for one: setup_inputs(seed, part) draws one part's arguments, and reference() takes and returns one part's arrays. A program takes and returns all parts, laid end to end along the dimension named above; an argument that names none is the same for every part. Nothing has to cross between parts.
Inputs may be any that keep to these rules, and one draw needn't show every extreme that they name: `segment_ids`: document numbers never fall along the sequence; each document holds 1 to 2048 positions and one holds exactly 2048.
All inputs are finite; a program needn't handle non-finite values.
Results may differ from the reference program's by a relative error of at most 0.014.
Values may be sent and summed in bfloat16 or wider, within the bound.
A program may use at most 64 MiB of HBM per device.

```python
import math
import jax
import jax.numpy as jnp
import numpy as np

D = 1024
F = 64
BLK = 256
SEQ_DEV = 2048
TOKENS = 8192
GRP = 8
SECTIONS = 2
N_SEQ = 4


def block_levels(stream_key, dims, shards, smallest, top_value):
    loudness = 1.0
    for position, blocks in shards:
        draws = jax.random.uniform(jax.random.fold_in(jax.random.fold_in(stream_key, 6), position), (blocks,), jnp.float32, smallest / len(shards), top_value / len(shards))
        loudness = loudness * jnp.repeat(jnp.exp(draws), dims[position] // blocks).reshape((-1,) + (1,) * (len(dims) - 1 - position))
    return loudness


def profile(number_of, total, limit, slope):
    loads = [(1 << 20) // math.isqrt(rank ** slope) + 1 for rank in range(2, number_of + 1)]
    surplus, counts = total - limit - (number_of - 1), [1] * (number_of - 1)
    while surplus > 0:
        candidates = [i for i in range(number_of - 1) if counts[i] < limit]
        mass, left = sum([loads[i] for i in candidates]), surplus
        for i in candidates:
            extra = min(limit - counts[i], max(1, left * loads[i] // mass), surplus)
            counts[i] = counts[i] + extra
            surplus = surplus - extra
    return np.array([limit] + counts)


def uneven(own_key, number_of, total, limit, skew):
    if number_of == 2:
        one = jax.random.randint(own_key, (), max(1, total - limit), min(limit, total - 1) + 1)
        return jnp.stack([one, total - one])
    tallies = jnp.asarray(profile(number_of, total, limit, skew), jnp.int32)
    twos = (number_of - 1) // 2
    giver, taker = tallies[1:1 + 2 * twos:2], tallies[2:2 + 2 * twos:2]
    slack = jnp.minimum(giver - 1, limit - taker)
    moved = jax.random.randint(jax.random.fold_in(own_key, 1), (twos,), 0, 1 << 20) % (slack + 1)
    tallies = tallies.at[1:1 + 2 * twos:2].set(giver - moved).at[2:2 + 2 * twos:2].set(taker + moved)
    return tallies[jax.random.permutation(jax.random.fold_in(own_key, 2), number_of)]


def noise(stream_key, extent, width, most, cuts=(), kind=jnp.bfloat16):
    level = block_levels(stream_key, extent, cuts, -0.22, 0.18) if cuts else 1.0
    array = jax.random.normal(stream_key, extent, jnp.float32) * width * level
    return jnp.minimum(jnp.maximum(array, -most), most).astype(kind)


def setup_inputs(seed: int = 0, part: int = 0) -> dict:
    keys = jax.random.split(jax.random.key(seed), 13)
    part_splits = jax.random.split(jax.random.fold_in(keys[12], part), 13)
    return {
        "query": noise(part_splits[0], (TOKENS, D), 1.0, 6.0, ((0, 4), (1, 4))),
        "keyed": noise(part_splits[1], (TOKENS, D), 1.0, 6.0, ((0, 4), (1, 4))),
        "values": noise(part_splits[2], (TOKENS, D), 1.0, 6.0, ((0, 4), (1, 4))),
        "cotangent": noise(part_splits[3], (TOKENS, D), 1.0, 6.0, ((0, 4), (1, 4))),
        "segment_ids": jnp.searchsorted(jnp.cumsum(uneven(part_splits[4], 2 * N_SEQ, TOKENS, SEQ_DEV, 0)), jnp.arange(TOKENS), side="right").astype(jnp.int32),
        "positions": noise(part_splits[5], (TOKENS, F), 1.0, 6.0, ((0, 4),)),
        "filter_weight": noise(keys[6], (F, D), F ** -0.5, 0.75, ((0, 4), (1, 4))),
        "skip_gain": jnp.clip(0.5 + 1.0 * jax.random.uniform(keys[7], (D,), jnp.float32) ** block_levels(keys[7], (D,), ((0, 4),), -0.2, 0.2), 0.5, 1.5),
        "first_factor": noise(keys[8], (BLK, BLK), BLK ** -0.5, 0.375),
        "second_factor": noise(keys[9], (GRP, GRP), GRP ** -0.5, 2.0),
        "self_coef": noise(keys[10], (SECTIONS, N_SEQ, SEQ_DEV), 0.7, 4.0, ((1, 4),)),
        "cross_coef": noise(keys[11], (SECTIONS, N_SEQ, SEQ_DEV), 0.7, 4.0, ((1, 4),)),
    }


def factor_one(x, first, transposed):
    x3 = x.reshape(TOKENS // BLK, BLK, x.shape[1]).astype(jnp.float32)
    if transposed:
        y = jnp.einsum('jcd,bc->jbd', x3, first.astype(jnp.float32))
    else:
        y = jnp.einsum('jbd,bc->jcd', x3, first.astype(jnp.float32))
    return y.astype(jnp.bfloat16).reshape(x.shape)


def factor_two(x, second, transposed):
    x4 = x.reshape(N_SEQ, GRP, BLK, x.shape[1]).astype(jnp.float32)
    if transposed:
        y = jnp.einsum('nibd,ji->njbd', x4, second.astype(jnp.float32))
    else:
        y = jnp.einsum('njbd,ji->nibd', x4, second.astype(jnp.float32))
    return y.astype(jnp.bfloat16).reshape(x.shape)


def butterfly(x, self_coef, cross_coef, section, transposed):
    x3 = x.reshape(N_SEQ, SEQ_DEV, x.shape[1])
    partner = jnp.bitwise_xor(jnp.arange(N_SEQ, dtype=jnp.int32), jnp.int32(1 << section))
    other = x3[partner]
    own_c = self_coef[section].astype(jnp.float32)
    cross = cross_coef[section]
    if transposed:
        cross = cross[partner]
    cross = cross.astype(jnp.float32)
    y = own_c[:, :, None] * x3.astype(jnp.float32) + cross[:, :, None] * other.astype(jnp.float32)
    return y.astype(jnp.bfloat16).reshape(x.shape)


def monarch(x, first, second, self_coef, cross_coef):
    x = factor_one(x, first, False)
    x = factor_two(x, second, False)
    for section in range(SECTIONS):
        x = butterfly(x, self_coef, cross_coef, section, False)
    return x


def monarch_t(x, first, second, self_coef, cross_coef):
    for section in reversed(range(SECTIONS)):
        x = butterfly(x, self_coef, cross_coef, section, True)
    x = factor_two(x, second, True)
    return factor_one(x, first, True)


def reference(query, keyed, values, cotangent, segment_ids, positions, filter_weight, skip_gain, first_factor, second_factor, self_coef, cross_coef):
    before = jnp.concatenate([jnp.full((1,), -1, jnp.int32), segment_ids[:-1].astype(jnp.int32)])
    keep = (segment_ids.astype(jnp.int32) == before).astype(jnp.float32)[:, None]
    u = (keyed.astype(jnp.float32) * values.astype(jnp.float32) * keep).astype(jnp.bfloat16)
    filt = jnp.dot(positions, filter_weight, preferred_element_type=jnp.float32)
    z = monarch(u, first_factor, second_factor, self_coef, cross_coef)
    w = (filt * z.astype(jnp.float32)).astype(jnp.bfloat16)
    conv = monarch_t(w, first_factor, second_factor, self_coef, cross_coef)
    total = conv.astype(jnp.float32) + skip_gain[None, :] * u.astype(jnp.float32)
    mixed = (query.astype(jnp.float32) * total).astype(jnp.bfloat16)
    grad_query = (cotangent.astype(jnp.float32) * total).astype(jnp.bfloat16)
    gt = (cotangent.astype(jnp.float32) * query.astype(jnp.float32)).astype(jnp.bfloat16)
    dw = monarch(gt, first_factor, second_factor, self_coef, cross_coef)
    dfilt = (dw.astype(jnp.float32) * z.astype(jnp.float32)).astype(jnp.bfloat16)
    scale = float(TOKENS) ** -0.5
    grad_filter = jnp.dot(positions.T, dfilt, preferred_element_type=jnp.float32) * scale
    dz = (dw.astype(jnp.float32) * filt).astype(jnp.bfloat16)
    back = monarch_t(dz, first_factor, second_factor, self_coef, cross_coef)
    du = back.astype(jnp.float32) + skip_gain[None, :] * gt.astype(jnp.float32)
    grad_keyed = (du * keep * values.astype(jnp.float32)).astype(jnp.bfloat16)
    grad_values = (du * keep * keyed.astype(jnp.float32)).astype(jnp.bfloat16)
    return mixed, grad_query, grad_keyed, grad_values, grad_filter
```

```python
import functools
import math

import jax
import jax.numpy as jnp
from jax import lax
from jax.experimental import pallas as pl
from jax.experimental.pallas import tpu as pltpu
from jax.sharding import PartitionSpec as P

BLK = 256
LANES = 128
F32 = jnp.float32
BF16 = jnp.bfloat16


def kernel(
    count, sections, scale,
    query, keyed, values, cotangent, keep_in, ends, pos, weight, gain, first, second, coefs,
    mixed, grad_query, grad_keyed, grad_values, grad_filter,
    first_t, keep_t, u_all, gt_all, half, fwd_send, fwd_recv, back_send, back_recv,
    pos_send, pos_recv, weight_send, weight_recv, ends_recv, coef_recv, coef_t,
    weight_lo, weight_hi, filt, dw_keep, dfilt, part_send, part_recv,
    field_send_sem, field_recv_sem, small_send_sem, small_recv_sem, ends_sem,
):
    rows, width = query.shape
    groups = rows // BLK
    quarter = rows // count
    packed = quarter // 2
    feats = pos.shape[1]
    share = weight.shape[0]
    chunks = width // LANES
    me = lax.axis_index("seq")
    others = [(k, lax.rem(me + k, count)) for k in range(1, count)]
    sources = [(k, lax.rem(me + count - k, count)) for k in range(1, count)]

    barrier = pltpu.get_barrier_semaphore()
    for _, other in others:
        pl.semaphore_signal(barrier, inc=1, device_id={"seq": other}, device_id_type=pl.DeviceIdType.MESH)

    def remote(src, dst, send, recv, other):
        return pltpu.make_async_remote_copy(
            src_ref=src, dst_ref=dst, send_sem=send, recv_sem=recv,
            device_id={"seq": other}, device_id_type=pl.DeviceIdType.MESH,
        )

    for p in range(count):
        block = pos[p * quarter:(p + 1) * quarter, :]
        pos_send[p] = jnp.concatenate([block[:packed], block[packed:]], axis=1)
    weight_send[...] = weight[...].astype(F32)
    first_t[...] = first[...].astype(F32).T.astype(BF16)

    pl.semaphore_wait(barrier, count - 1)

    def small(kind, k, other):
        send, recv = small_send_sem.at[kind, k], small_recv_sem.at[kind, k]
        if kind == 0:
            return remote(pos_send.at[other], pos_recv.at[me], send, recv, other)
        if kind == 1:
            return remote(weight_send, weight_recv.at[me], send, recv, other)
        if kind == 2:
            return remote(coefs.at[other], coef_recv.at[me], send, recv, other)
        return remote(part_send.at[other], part_recv.at[me], send, recv, other)

    ring = remote(ends.at[1], ends_recv, ends_sem.at[0], ends_sem.at[1], lax.rem(me + 1, count))
    ring.start()
    for kind in (2, 1, 0):
        for k, other in others:
            small(kind, k, other).start()
    pos_recv[me] = pos_send[me]
    weight_recv[me] = weight_send[...]
    coef_recv[me] = coefs[me]

    def forward_copy(unit, k, other):
        return remote(
            fwd_send.at[unit, other], fwd_recv.at[unit, me],
            field_send_sem.at[0, unit, k], field_recv_sem.at[0, unit, k], other,
        )

    def back_copy(unit, k, other):
        return remote(
            back_send.at[unit, other], back_recv.at[unit, me],
            field_send_sem.at[1, unit, k], field_recv_sem.at[1, unit, k], other,
        )

    def lanes(chunk):
        return slice(chunk * LANES, (chunk + 1) * LANES)

    step = min(16, quarter)
    mat = [[second[j, i] for i in range(groups)] for j in range(groups)]

    def forward(unit, chunk, source):
        for j in range(groups):
            x = source[j * BLK:(j + 1) * BLK, lanes(chunk)]
            half[j] = jnp.dot(first_t[...], x, preferred_element_type=F32).astype(BF16)

        @pl.loop(0, BLK // step)
        def _(r):
            at = pl.multiple_of(r * step, step)
            xs = [half[j, pl.ds(at, step), :].astype(F32) for j in range(groups)]
            for i in range(groups):
                y = mat[0][i] * xs[0]
                for j in range(1, groups):
                    y = y + mat[j][i] * xs[j]
                place = i * BLK + at
                fwd_send[unit, place // quarter, pl.ds(pl.multiple_of(lax.rem(place, quarter), step), step), :] = y.astype(BF16)

        for k, other in others:
            forward_copy(unit, k, other).start()
        fwd_recv[unit, me] = fwd_send[unit, me]

    for j in range(groups):
        at = slice(j * BLK, (j + 1) * BLK)
        gt_all[at, :] = (cotangent[at, :].astype(F32) * query[at, :].astype(F32)).astype(BF16)
    for chunk in range(chunks):
        forward(chunk, chunk, gt_all)

    ring.wait_recv()
    same = jnp.where((ends[0] == ends_recv[...]) & (me > 0), 1.0, 0.0)
    spot = (lax.broadcasted_iota(jnp.int32, keep_in.shape, 0) == 0) & (lax.broadcasted_iota(jnp.int32, keep_in.shape, 1) == 0)
    keep_t[...] = jnp.where(spot, same, keep_in[...]).T
    for j in range(groups):
        at = slice(j * BLK, (j + 1) * BLK)
        u_all[at, :] = (keyed[at, :].astype(F32) * values[at, :].astype(F32) * keep_t[:, j:j + 1]).astype(BF16)
    for chunk in range(chunks):
        forward(chunks + chunk, chunk, u_all)

    for kind in (2, 1, 0):
        for k, source in sources:
            small(kind, k, source).wait_recv()
    weight_lo[...] = jnp.zeros_like(weight_lo)
    weight_hi[...] = jnp.zeros_like(weight_hi)
    for p in range(count):
        weight_lo[p * share:(p + 1) * share, :] = weight_recv[p]
        weight_hi[feats + p * share:feats + (p + 1) * share, :] = weight_recv[p]
    low, high = weight_lo[...].astype(BF16), weight_hi[...].astype(BF16)
    for p in range(count):
        filt[p, :packed, :] = jnp.dot(pos_recv[p], low, preferred_element_type=F32)
        filt[p, packed:, :] = jnp.dot(pos_recv[p], high, preferred_element_type=F32)
        coef_t[p] = coef_recv[p].T

    def rounded(x):
        return x.astype(BF16).astype(F32)

    def middle(unit, chunk, gated):
        for k, source in sources:
            forward_copy(unit, k, source).wait_recv()

        @pl.loop(0, quarter // step)
        def _(r):
            at = pl.ds(pl.multiple_of(r * step, step), step)
            xs = [fwd_recv[unit, p, at, :].astype(F32) for p in range(count)]
            cols = [coef_t[p, at, :] for p in range(count)]

            def own(k, p):
                return cols[p][:, k:k + 1]

            def cross(k, p):
                return cols[p][:, sections + k:sections + k + 1]

            for k in range(sections):
                xs = [rounded(own(k, p) * xs[p] + cross(k, p) * xs[p ^ (1 << k)]) for p in range(count)]
            for p in range(count):
                if gated:
                    dw_keep[chunk, p, at, :] = xs[p].astype(BF16)
                else:
                    dfilt[p, at, :] = (dw_keep[chunk, p, at, :].astype(F32) * xs[p]).astype(BF16)
            xs = [rounded(xs[p] * filt[p, at, lanes(chunk)]) for p in range(count)]
            for k in reversed(range(sections)):
                xs = [
                    rounded(own(k, p) * xs[p] + cross(k, p ^ (1 << k)) * xs[p ^ (1 << k)])
                    for p in range(count)
                ]
            for p in range(count):
                back_send[unit, p, at, :] = xs[p].astype(BF16)

        for k, other in others:
            back_copy(unit, k, other).start()
        back_recv[unit, me] = back_send[unit, me]
        if not gated:
            over = (((0,), (0,)), ((), ()))
            lo = jnp.zeros((2 * feats, LANES), F32)
            hi = jnp.zeros((2 * feats, LANES), F32)
            for p in range(count):
                lo = lo + lax.dot_general(pos_recv[p], dfilt[p, :packed, :], over, preferred_element_type=F32)
                hi = hi + lax.dot_general(pos_recv[p], dfilt[p, packed:, :], over, preferred_element_type=F32)
            total = (lo[:feats] + hi[feats:]) * scale
            for p in range(count):
                part_send[p, :, lanes(chunk)] = total[p * share:(p + 1) * share]

    for chunk in range(chunks):
        middle(chunk, chunk, True)
    for chunk in range(chunks):
        middle(chunks + chunk, chunk, False)
    for k, other in others:
        small(3, k, other).start()
    part_recv[me] = part_send[me]

    def final(unit, chunk, gated):
        for k, source in sources:
            back_copy(unit, k, source).wait_recv()

        @pl.loop(0, BLK // step)
        def _(r):
            at = pl.multiple_of(r * step, step)
            xs = []
            for i in range(groups):
                place = i * BLK + at
                xs.append(back_recv[unit, place // quarter, pl.ds(pl.multiple_of(lax.rem(place, quarter), step), step), :].astype(F32))
            for j in range(groups):
                y = mat[j][0] * xs[0]
                for i in range(1, groups):
                    y = y + mat[j][i] * xs[i]
                half[j, pl.ds(at, step), :] = y.astype(BF16)

        skip = gain[0:1, lanes(chunk)]
        cut = lanes(chunk)
        for j in range(groups):
            at = slice(j * BLK, (j + 1) * BLK)
            y = rounded(jnp.dot(first[...], half[j], preferred_element_type=F32))
            if gated:
                du = (y + skip * gt_all[at, cut].astype(F32)) * keep_t[:, j:j + 1]
                grad_keyed[at, cut] = (du * values[at, cut].astype(F32)).astype(BF16)
                grad_values[at, cut] = (du * keyed[at, cut].astype(F32)).astype(BF16)
            else:
                total = y + skip * u_all[at, cut].astype(F32)
                mixed[at, cut] = (query[at, cut].astype(F32) * total).astype(BF16)
                grad_query[at, cut] = (cotangent[at, cut].astype(F32) * total).astype(BF16)

    for chunk in range(chunks):
        final(chunk, chunk, True)
    for chunk in range(chunks):
        final(chunks + chunk, chunk, False)

    for k, source in sources:
        small(3, k, source).wait_recv()
    total = part_recv[0]
    for p in range(1, count):
        total = total + part_recv[p]
    grad_filter[...] = total

    ring.wait_send()
    for k, other in others:
        for kind in range(4):
            small(kind, k, other).wait_send()
        for unit in range(2 * chunks):
            forward_copy(unit, k, other).wait_send()
            back_copy(unit, k, other).wait_send()


def on_device(
    query, keyed, values, cotangent, segment_ids, positions, filter_weight, skip_gain,
    first_factor, second_factor, self_coef, cross_coef,
):
    count = lax.axis_size("seq")
    sections = self_coef.shape[0]
    rows, width = query.shape
    groups = rows // BLK
    quarter = rows // count
    feats = positions.shape[1]
    share = filter_weight.shape[0]
    chunks = width // LANES
    units = 2 * chunks
    kinds = -(-2 * sections // 8) * 8
    before = jnp.concatenate([segment_ids[:1], segment_ids[:-1]])
    keep = (segment_ids == before).astype(F32).reshape(groups, BLK)
    ends = jnp.broadcast_to(jnp.stack([segment_ids[0], segment_ids[-1]])[:, None, None], (2, groups, BLK))
    coefs = jnp.concatenate([self_coef[:, 0], cross_coef[:, 0]]).astype(F32)
    coefs = jnp.pad(coefs, ((0, kinds - 2 * sections), (0, 0)))
    coefs = coefs.reshape(kinds, count, quarter).transpose(1, 0, 2)
    scale = 1.0 / math.sqrt(rows * count)
    vmem = pl.BlockSpec(memory_space=pltpu.VMEM)
    smem = pl.BlockSpec(memory_space=pltpu.SMEM)
    field = jax.ShapeDtypeStruct((rows, width), BF16)
    return pl.pallas_call(
        functools.partial(kernel, count, sections, scale),
        out_shape=(field, field, field, field, jax.ShapeDtypeStruct((share, width), F32)),
        in_specs=[vmem] * 10 + [smem, vmem],
        out_specs=(vmem,) * 5,
        scratch_shapes=[
            pltpu.VMEM((BLK, BLK), BF16),
            pltpu.VMEM((BLK, groups), F32),
            pltpu.VMEM((rows, width), BF16),
            pltpu.VMEM((rows, width), BF16),
            pltpu.VMEM((groups, BLK, LANES), BF16),
            pltpu.VMEM((units, count, quarter, LANES), BF16),
            pltpu.VMEM((units, count, quarter, LANES), BF16),
            pltpu.VMEM((units, count, quarter, LANES), BF16),
            pltpu.VMEM((units, count, quarter, LANES), BF16),
            pltpu.VMEM((count, quarter // 2, 2 * feats), BF16),
            pltpu.VMEM((count, quarter // 2, 2 * feats), BF16),
            pltpu.VMEM((share, width), F32),
            pltpu.VMEM((count, share, width), F32),
            pltpu.VMEM((groups, BLK), jnp.int32),
            pltpu.VMEM((count, kinds, quarter), F32),
            pltpu.VMEM((count, quarter, kinds), F32),
            pltpu.VMEM((2 * feats, width), F32),
            pltpu.VMEM((2 * feats, width), F32),
            pltpu.VMEM((count, quarter, width), F32),
            pltpu.VMEM((chunks, count, quarter, LANES), BF16),
            pltpu.VMEM((count, quarter, LANES), BF16),
            pltpu.VMEM((count, share, width), F32),
            pltpu.VMEM((count, share, width), F32),
            pltpu.SemaphoreType.DMA((2, units, count)),
            pltpu.SemaphoreType.DMA((2, units, count)),
            pltpu.SemaphoreType.DMA((4, count)),
            pltpu.SemaphoreType.DMA((4, count)),
            pltpu.SemaphoreType.DMA((2,)),
        ],
        compiler_params=pltpu.CompilerParams(
            collective_id=0, has_side_effects=True, vmem_limit_bytes=50 * 1024 * 1024
        ),
        cost_estimate=pl.CostEstimate(flops=2 * 10**9, bytes_accessed=8 * rows * width * 2, transcendentals=0),
    )(
        query, keyed, values, cotangent, keep, ends, positions, filter_weight,
        skip_gain[None, :], first_factor, second_factor.astype(F32), coefs,
    )


def solution(mesh):
    field = P(("groups", "seq"), "chan")
    return jax.shard_map(
        on_device,
        mesh=mesh,
        in_specs=(
            field, field, field, field, P(("groups", "seq")), P(("groups", "seq"), None),
            P("seq", "chan"), P("chan"), P(), P(), P(None, "seq", None), P(None, "seq", None),
        ),
        out_specs=(field,) * 5,
        check_vma=False,
    )
```

```python
import functools
import math

import jax
import jax.numpy as jnp
from jax import lax
from jax.experimental import pallas as pl
from jax.experimental.pallas import tpu as pltpu
from jax.sharding import PartitionSpec as P

BLK = 256
LANES = 128
F32 = jnp.float32
BF16 = jnp.bfloat16


def kernel(
    count, sections, scale,
    query_in, keyed_in, values_in, cotangent_in, ids, pos, weight, first, second, self_coef, cross_coef,
    conv, back, keep_out, part_recv,
    query, keyed, values, cotangent, first_t, keep_t, u_all, gt_all, half, fwd_send, fwd_recv, back_send, back_recv,
    pos_send, pos_recv, weight_send, weight_recv, ends_recv, coef_recv, coef_t,
    coef_send, weight_all, filt, dw_keep, dfilt, part_send,
    field_send_sem, field_recv_sem, small_send_sem, small_recv_sem, ends_sem, load_sem,
):
    rows, width = query.shape
    groups = rows // BLK
    quarter = rows // count
    share = weight.shape[0]
    chunks = width // LANES
    me = lax.axis_index("seq")
    others = [(k, lax.rem(me + k, count)) for k in range(1, count)]
    sources = [(k, lax.rem(me + count - k, count)) for k in range(1, count)]

    barrier = pltpu.get_barrier_semaphore()
    for _, other in others:
        pl.semaphore_signal(barrier, inc=1, device_id={"seq": other}, device_id_type=pl.DeviceIdType.MESH)

    def remote(src, dst, send, recv, other):
        return pltpu.make_async_remote_copy(
            src_ref=src, dst_ref=dst, send_sem=send, recv_sem=recv,
            device_id={"seq": other}, device_id_type=pl.DeviceIdType.MESH,
        )

    loads = []
    for chunk in range(chunks):
        cut = pl.ds(chunk * LANES, LANES)
        for n, (far, near) in enumerate(((query_in, query), (cotangent_in, cotangent), (keyed_in, keyed), (values_in, values))):
            loads.append(pltpu.make_async_copy(far.at[:, cut], near.at[:, cut], load_sem.at[chunk, n]))
    order = [4 * chunk + n for n0 in (0, 2) for chunk in range(chunks) for n in (n0, n0 + 1)]
    for at in order:
        loads[at].start()

    coef_send[...] = jnp.zeros_like(coef_send)
    for p in range(count):
        cut = slice(p * quarter, (p + 1) * quarter)
        pos_send[p] = pos[:, cut]
        coef_send[p, :sections, :] = self_coef[:, cut].astype(F32)
        coef_send[p, sections:2 * sections, :] = cross_coef[:, cut].astype(F32)
    weight_send[...] = weight[...].astype(F32)
    first_t[...] = first[...].astype(F32).T.astype(BF16)

    pl.semaphore_wait(barrier, count - 1)

    def small(kind, k, other):
        send, recv = small_send_sem.at[kind, k], small_recv_sem.at[kind, k]
        if kind == 0:
            return remote(pos_send.at[other], pos_recv.at[me], send, recv, other)
        if kind == 1:
            return remote(weight_send, weight_recv.at[me], send, recv, other)
        if kind == 2:
            return remote(coef_send.at[other], coef_recv.at[me], send, recv, other)
        return remote(part_send.at[other], part_recv.at[me], send, recv, other)

    ring = remote(ids, ends_recv, ends_sem.at[0], ends_sem.at[1], lax.rem(me + 1, count))
    ring.start()
    for kind in (2, 1, 0):
        for k, other in others:
            small(kind, k, other).start()
    pos_recv[me] = pos_send[me]
    weight_recv[me] = weight_send[...]
    coef_recv[me] = coef_send[me]

    def forward_copy(unit, k, other):
        return remote(
            fwd_send.at[unit, other], fwd_recv.at[unit, me],
            field_send_sem.at[0, unit, k], field_recv_sem.at[0, unit, k], other,
        )

    def back_copy(unit, k, other):
        return remote(
            back_send.at[unit, other], back_recv.at[unit, me],
            field_send_sem.at[1, unit, k], field_recv_sem.at[1, unit, k], other,
        )

    def lanes(chunk):
        return slice(chunk * LANES, (chunk + 1) * LANES)

    step = min(16, quarter)
    mat = [[second[j, i] for i in range(groups)] for j in range(groups)]

    def forward(unit, chunk, source):
        for j in range(groups):
            x = source[j * BLK:(j + 1) * BLK, lanes(chunk)]
            half[j] = jnp.dot(first_t[...], x, preferred_element_type=F32).astype(BF16)

        if quarter % BLK == 0:
            per = quarter // BLK
            for k, other in others + [(0, me)]:
                mats = [[second[j, other * per + i] for i in range(per)] for j in range(groups)]

                @pl.loop(0, BLK // step)
                def _(r, mats=mats, k=k, other=other):
                    at = pl.multiple_of(r * step, step)
                    xs = [half[j, pl.ds(at, step), :].astype(F32) for j in range(groups)]
                    for i in range(per):
                        y = mats[0][i] * xs[0]
                        for j in range(1, groups):
                            y = y + mats[j][i] * xs[j]
                        place = pl.ds(pl.multiple_of(i * BLK + at, step), step)
                        if k == 0:
                            fwd_recv[unit, me, place, :] = y.astype(BF16)
                        else:
                            fwd_send[unit, other, place, :] = y.astype(BF16)

                if k:
                    forward_copy(unit, k, other).start()
            return

        @pl.loop(0, BLK // step)
        def _(r):
            at = pl.multiple_of(r * step, step)
            xs = [half[j, pl.ds(at, step), :].astype(F32) for j in range(groups)]
            for i in range(groups):
                y = mat[0][i] * xs[0]
                for j in range(1, groups):
                    y = y + mat[j][i] * xs[j]
                place = i * BLK + at
                fwd_send[unit, place // quarter, pl.ds(pl.multiple_of(lax.rem(place, quarter), step), step), :] = y.astype(BF16)

        for k, other in others:
            forward_copy(unit, k, other).start()
        fwd_recv[unit, me] = fwd_send[unit, me]

    for chunk in range(chunks):
        loads[4 * chunk].wait()
        loads[4 * chunk + 1].wait()
        cut = lanes(chunk)
        for j in range(groups):
            at = slice(j * BLK, (j + 1) * BLK)
            gt_all[at, cut] = (cotangent[at, cut].astype(F32) * query[at, cut].astype(F32)).astype(BF16)
        forward(chunk, chunk, gt_all)

    ring.wait_recv()
    here = ids[...]
    above = jnp.concatenate([ends_recv[groups - 1:, BLK - 1:], here[:groups - 1, BLK - 1:]], axis=0)
    before = jnp.concatenate([above, here[:, :BLK - 1]], axis=1)
    spot = (lax.broadcasted_iota(jnp.int32, ids.shape, 0) == 0) & (lax.broadcasted_iota(jnp.int32, ids.shape, 1) == 0)
    keep = jnp.where((here == before) & ((me > 0) | jnp.logical_not(spot)), 1.0, 0.0)
    keep_out[...] = keep
    keep_t[...] = keep.T
    for chunk in range(chunks):
        loads[4 * chunk + 2].wait()
        loads[4 * chunk + 3].wait()
        cut = lanes(chunk)
        for j in range(groups):
            at = slice(j * BLK, (j + 1) * BLK)
            u_all[at, cut] = (keyed[at, cut].astype(F32) * values[at, cut].astype(F32) * keep_t[:, j:j + 1]).astype(BF16)
        forward(chunks + chunk, chunk, u_all)

    for kind in (2, 1, 0):
        for k, source in sources:
            small(kind, k, source).wait_recv()
    for p in range(count):
        weight_all[p * share:(p + 1) * share, :] = weight_recv[p]
    whole = weight_all[...].astype(BF16)
    for p in range(count):
        filt[p] = lax.dot_general(pos_recv[p], whole, (((0,), (0,)), ((), ())), preferred_element_type=F32)
        coef_t[p] = coef_recv[p].T

    def rounded(x):
        return x.astype(BF16).astype(F32)

    def middle(unit, chunk, gated):
        for k, source in sources:
            forward_copy(unit, k, source).wait_recv()

        @pl.loop(0, quarter // step)
        def _(r):
            at = pl.ds(pl.multiple_of(r * step, step), step)
            xs = [fwd_recv[unit, p, at, :].astype(F32) for p in range(count)]
            cols = [coef_t[p, at, :] for p in range(count)]

            def own(k, p):
                return cols[p][:, k:k + 1]

            def cross(k, p):
                return cols[p][:, sections + k:sections + k + 1]

            for k in range(sections):
                xs = [rounded(own(k, p) * xs[p] + cross(k, p) * xs[p ^ (1 << k)]) for p in range(count)]
            for p in range(count):
                if gated:
                    dw_keep[chunk, p, at, :] = xs[p].astype(BF16)
                else:
                    dfilt[p, at, :] = (dw_keep[chunk, p, at, :].astype(F32) * xs[p]).astype(BF16)
            xs = [rounded(xs[p] * filt[p, at, lanes(chunk)]) for p in range(count)]
            for k in reversed(range(sections)):
                xs = [
                    rounded(own(k, p) * xs[p] + cross(k, p ^ (1 << k)) * xs[p ^ (1 << k)])
                    for p in range(count)
                ]
            for p in range(count):
                back_send[unit, p, at, :] = xs[p].astype(BF16)

        for k, other in others:
            back_copy(unit, k, other).start()
        back_recv[unit, me] = back_send[unit, me]
        if not gated:
            total = jnp.dot(pos_recv[0], dfilt[0], preferred_element_type=F32)
            for p in range(1, count):
                total = total + jnp.dot(pos_recv[p], dfilt[p], preferred_element_type=F32)
            total = total * scale
            for p in range(count):
                part_send[p, :, lanes(chunk)] = total[p * share:(p + 1) * share]

    for chunk in range(chunks):
        middle(chunk, chunk, True)
    for chunk in range(chunks):
        middle(chunks + chunk, chunk, False)
    for k, other in others:
        small(3, k, other).start()
    part_recv[me] = part_send[me]

    def final(unit, chunk, target):
        for k, source in sources:
            back_copy(unit, k, source).wait_recv()

        @pl.loop(0, BLK // step)
        def _(r):
            at = pl.multiple_of(r * step, step)
            xs = []
            for i in range(groups):
                place = i * BLK + at
                xs.append(back_recv[unit, place // quarter, pl.ds(pl.multiple_of(lax.rem(place, quarter), step), step), :].astype(F32))
            for j in range(groups):
                y = mat[j][0] * xs[0]
                for i in range(1, groups):
                    y = y + mat[j][i] * xs[i]
                half[j, pl.ds(at, step), :] = y.astype(BF16)

        for j in range(groups):
            target[j * BLK:(j + 1) * BLK, lanes(chunk)] = jnp.dot(
                first[...], half[j], preferred_element_type=F32
            ).astype(BF16)

    for chunk in range(chunks):
        final(chunk, chunk, back)
    for chunk in range(chunks):
        final(chunks + chunk, chunk, conv)

    for k, source in sources:
        small(3, k, source).wait_recv()
    ring.wait_send()
    for k, other in others:
        for kind in range(4):
            small(kind, k, other).wait_send()
        for unit in range(2 * chunks):
            forward_copy(unit, k, other).wait_send()
            back_copy(unit, k, other).wait_send()


def finish(
    query, keyed, values, cotangent, conv, back, keep, gain, parts,
    mixed, grad_query, grad_keyed, grad_values, grad_filter,
):
    keep_t = keep[...].T
    lane = lax.broadcasted_iota(jnp.int32, keep_t.shape, 1)
    kept = jnp.sum(jnp.where(lane == pl.program_id(0), keep_t, 0.0), axis=1, keepdims=True)
    q, c = query[...].astype(F32), cotangent[...].astype(F32)
    k, v = keyed[...].astype(F32), values[...].astype(F32)
    skip = gain[...]
    u = (k * v * kept).astype(BF16).astype(F32)
    total = conv[...].astype(F32) + skip * u
    mixed[...] = (q * total).astype(BF16)
    grad_query[...] = (c * total).astype(BF16)
    gated = (c * q).astype(BF16).astype(F32)
    du = (back[...].astype(F32) + skip * gated) * kept
    grad_keyed[...] = (du * v).astype(BF16)
    grad_values[...] = (du * k).astype(BF16)

    @pl.when(pl.program_id(0) == 0)
    def _():
        total = parts[0]
        for p in range(1, parts.shape[0]):
            total = total + parts[p]
        grad_filter[...] = total


def on_device(
    query, keyed, values, cotangent, segment_ids, positions, filter_weight, skip_gain,
    first_factor, second_factor, self_coef, cross_coef,
):
    count = lax.axis_size("seq")
    sections = self_coef.shape[0]
    rows, width = query.shape
    groups = rows // BLK
    quarter = rows // count
    feats = positions.shape[1]
    share = filter_weight.shape[0]
    chunks = width // LANES
    units = 2 * chunks
    kinds = -(-2 * sections // 8) * 8
    scale = 1.0 / math.sqrt(rows * count)
    vmem = pl.BlockSpec(memory_space=pltpu.VMEM)
    smem = pl.BlockSpec(memory_space=pltpu.SMEM)
    field = jax.ShapeDtypeStruct((rows, width), BF16)
    conv, back, keep, parts = pl.pallas_call(
        functools.partial(kernel, count, sections, scale),
        out_shape=(
            field, field, jax.ShapeDtypeStruct((groups, BLK), F32),
            jax.ShapeDtypeStruct((count, share, width), F32),
        ),
        in_specs=[pl.BlockSpec(memory_space=pl.ANY)] * 4 + [vmem] * 4 + [smem, vmem, vmem],
        out_specs=(vmem,) * 4,
        scratch_shapes=[
            pltpu.VMEM((rows, width), BF16),
            pltpu.VMEM((rows, width), BF16),
            pltpu.VMEM((rows, width), BF16),
            pltpu.VMEM((rows, width), BF16),
            pltpu.VMEM((BLK, BLK), BF16),
            pltpu.VMEM((BLK, groups), F32),
            pltpu.VMEM((rows, width), BF16),
            pltpu.VMEM((rows, width), BF16),
            pltpu.VMEM((groups, BLK, LANES), BF16),
            pltpu.VMEM((units, count, quarter, LANES), BF16),
            pltpu.VMEM((units, count, quarter, LANES), BF16),
            pltpu.VMEM((units, count, quarter, LANES), BF16),
            pltpu.VMEM((units, count, quarter, LANES), BF16),
            pltpu.VMEM((count, feats, quarter), BF16),
            pltpu.VMEM((count, feats, quarter), BF16),
            pltpu.VMEM((share, width), F32),
            pltpu.VMEM((count, share, width), F32),
            pltpu.VMEM((groups, BLK), jnp.int32),
            pltpu.VMEM((count, kinds, quarter), F32),
            pltpu.VMEM((count, quarter, kinds), F32),
            pltpu.VMEM((count, kinds, quarter), F32),
            pltpu.VMEM((feats, width), F32),
            pltpu.VMEM((count, quarter, width), F32),
            pltpu.VMEM((chunks, count, quarter, LANES), BF16),
            pltpu.VMEM((count, quarter, LANES), BF16),
            pltpu.VMEM((count, share, width), F32),
            pltpu.SemaphoreType.DMA((2, units, count)),
            pltpu.SemaphoreType.DMA((2, units, count)),
            pltpu.SemaphoreType.DMA((4, count)),
            pltpu.SemaphoreType.DMA((4, count)),
            pltpu.SemaphoreType.DMA((2,)),
            pltpu.SemaphoreType.DMA((chunks, 4)),
        ],
        compiler_params=pltpu.CompilerParams(
            collective_id=0, has_side_effects=True, vmem_limit_bytes=50 * 1024 * 1024
        ),
        cost_estimate=pl.CostEstimate(flops=2 * 10**9, bytes_accessed=8 * rows * width * 2, transcendentals=0),
    )(
        query, keyed, values, cotangent, segment_ids.reshape(groups, BLK), positions.T, filter_weight,
        first_factor, second_factor.astype(F32), self_coef[:, 0], cross_coef[:, 0],
    )
    block = pl.BlockSpec((BLK, width), lambda j: (j, 0))

    def full(*shape):
        return pl.BlockSpec(shape, lambda j: (0,) * len(shape))

    return pl.pallas_call(
        finish,
        grid=(groups,),
        out_shape=(field, field, field, field, jax.ShapeDtypeStruct((share, width), F32)),
        in_specs=[block] * 6 + [full(groups, BLK), full(1, width), full(count, share, width)],
        out_specs=(block, block, block, block, full(share, width)),
    )(query, keyed, values, cotangent, conv, back, keep, skip_gain[None, :], parts)


def solution(mesh):
    field = P(("groups", "seq"), "chan")
    return jax.shard_map(
        on_device,
        mesh=mesh,
        in_specs=(
            field, field, field, field, P(("groups", "seq")), P(("groups", "seq"), None),
            P("seq", "chan"), P("chan"), P(), P(), P(None, "seq", None), P(None, "seq", None),
        ),
        out_specs=(field,) * 5,
        check_vma=False,
    )
```

```python
import functools
import math

import jax
import jax.numpy as jnp
from jax import lax
from jax.experimental import pallas as pl
from jax.experimental.pallas import tpu as pltpu
from jax.sharding import PartitionSpec as P

BLK = 256
LANES = 128
F32 = jnp.float32
BF16 = jnp.bfloat16


def kernel(
    count, sections, scale,
    query_in, keyed_in, values_in, cotangent_in, ids_in, pos_in, weight_in, gain_in, first_in, second_in,
    self_in, cross_in,
    mixed_out, query_out, keyed_out, values_out, grad_filter,
    mixed, grad_query, grad_keyed, grad_values, ids, pos, weight, gain, first, second, self_coef, cross_coef, mat, part_recv,
    query, keyed, values, cotangent, first_t, keep_t, u_all, gt_all, half, fwd_send, fwd_recv, back_send, back_recv,
    pos_send, pos_recv, weight_send, weight_recv, ends_recv, coef_recv, coef_t,
    coef_send, weight_all, filt, dw_keep, dfilt, part_send,
    field_send_sem, field_recv_sem, small_send_sem, small_recv_sem, ends_sem, load_sem, tiny_sem, share_send_sem, share_recv_sem, store_sem,
):
    rows, width = query.shape
    groups = rows // BLK
    quarter = rows // count
    share = weight.shape[0]
    chunks = width // LANES
    me = lax.axis_index("seq")
    others = [(k, lax.rem(me + k, count)) for k in range(1, count)]
    sources = [(k, lax.rem(me + count - k, count)) for k in range(1, count)]
    feats = pos_in.shape[0]
    crew = lax.axis_size("chan")
    split = crew if (feats // crew) % 16 == 0 else 1
    part = feats // split
    spot = lax.axis_index("chan")
    if split > 1:
        mine = pl.ds(pl.multiple_of(spot * part, part), part)
        peers = [(k, lax.rem(spot + k, crew)) for k in range(1, crew)]
    else:
        mine, peers = slice(None), []

    barrier = pltpu.get_barrier_semaphore()
    for _, other in others:
        pl.semaphore_signal(barrier, inc=1, device_id={"seq": other}, device_id_type=pl.DeviceIdType.MESH)
    for _, peer in peers:
        pl.semaphore_signal(barrier, inc=1, device_id={"chan": peer}, device_id_type=pl.DeviceIdType.MESH)

    def remote(src, dst, send, recv, other, axis="seq"):
        return pltpu.make_async_remote_copy(
            src_ref=src, dst_ref=dst, send_sem=send, recv_sem=recv,
            device_id={axis: other}, device_id_type=pl.DeviceIdType.MESH,
        )

    loads = []
    for chunk in range(chunks):
        cut = pl.ds(chunk * LANES, LANES)
        for n, (far, near) in enumerate(((query_in, query), (cotangent_in, cotangent), (keyed_in, keyed), (values_in, values))):
            loads.append(pltpu.make_async_copy(far.at[:, cut], near.at[:, cut], load_sem.at[chunk, n]))
    order = [4 * chunk + n for n0 in (0, 2) for chunk in range(chunks) for n in (n0, n0 + 1)]
    tiny = [
        pltpu.make_async_copy(far, near, tiny_sem.at[n])
        for n, (far, near) in enumerate((
            (pos_in, pos), (self_in, self_coef), (cross_in, cross_coef), (weight_in, weight), (ids_in, ids),
            (first_in, first), (second_in, second), (gain_in, gain),
        ))
    ]
    for copy in tiny:
        copy.start()
    for at in order:
        loads[at].start()
    for copy in tiny:
        copy.wait()

    coef_send[...] = jnp.zeros_like(coef_send)
    for p in range(count):
        cut = slice(p * quarter, (p + 1) * quarter)
        pos_send[p] = pos[:, cut]
        coef_send[p, :sections, :] = self_coef[:, cut].astype(F32)
        coef_send[p, sections:2 * sections, :] = cross_coef[:, cut].astype(F32)
    weight_send[...] = weight[...].astype(F32)

    pl.semaphore_wait(barrier, count - 1 + len(peers))

    def small(kind, k, other):
        send, recv = small_send_sem.at[kind, k], small_recv_sem.at[kind, k]
        if kind == 0:
            return remote(pos_send.at[other, mine], pos_recv.at[me, mine], send, recv, other)
        if kind == 1:
            return remote(weight_send, weight_recv.at[me], send, recv, other)
        if kind == 2:
            return remote(coef_send.at[other], coef_recv.at[me], send, recv, other)
        return remote(part_send.at[other], part_recv.at[me], send, recv, other)

    ring = remote(ids, ends_recv, ends_sem.at[0], ends_sem.at[1], lax.rem(me + 1, count))
    ring.start()
    for kind in (2, 1, 0):
        for k, other in others:
            small(kind, k, other).start()
    pos_recv[me, mine] = pos_send[me, mine]
    weight_recv[me] = weight_send[...]
    coef_recv[me] = coef_send[me]

    def share_copy(k, peer):
        return remote(
            pos_recv.at[:, mine], pos_recv.at[:, mine], share_send_sem.at[k], share_recv_sem.at[k], peer, "chan",
        )

    def forward_copy(unit, k, other):
        return remote(
            fwd_send.at[unit, other], fwd_recv.at[unit, me],
            field_send_sem.at[0, unit, k], field_recv_sem.at[0, unit, k], other,
        )

    def back_copy(unit, k, other):
        return remote(
            back_send.at[unit, other], back_recv.at[unit, me],
            field_send_sem.at[1, unit, k], field_recv_sem.at[1, unit, k], other,
        )

    def lanes(chunk):
        return slice(chunk * LANES, (chunk + 1) * LANES)

    step = min(16, quarter)
    first_t[...] = first[...].astype(F32).T.astype(BF16)
    table = second[...].astype(F32)
    for j in range(groups):
        for i in range(groups):
            mat[j, i] = jnp.broadcast_to(table[j:j + 1, i:i + 1], mat.shape[2:])

    def forward(unit, chunk, source):
        for j in range(groups):
            x = source[j * BLK:(j + 1) * BLK, lanes(chunk)]
            half[j] = jnp.dot(first_t[...], x, preferred_element_type=F32).astype(BF16)

        if quarter % BLK == 0:
            per = quarter // BLK
            for k, other in others + [(0, me)]:
                mats = [[mat[j, other * per + i] for i in range(per)] for j in range(groups)]

                @pl.loop(0, BLK // step)
                def _(r, mats=mats, k=k, other=other):
                    at = pl.multiple_of(r * step, step)
                    xs = [half[j, pl.ds(at, step), :].astype(F32) for j in range(groups)]
                    for i in range(per):
                        y = mats[0][i] * xs[0]
                        for j in range(1, groups):
                            y = y + mats[j][i] * xs[j]
                        place = pl.ds(pl.multiple_of(i * BLK + at, step), step)
                        if k == 0:
                            fwd_recv[unit, me, place, :] = y.astype(BF16)
                        else:
                            fwd_send[unit, other, place, :] = y.astype(BF16)

                if k:
                    forward_copy(unit, k, other).start()
            return

        @pl.loop(0, BLK // step)
        def _(r):
            at = pl.multiple_of(r * step, step)
            xs = [half[j, pl.ds(at, step), :].astype(F32) for j in range(groups)]
            for i in range(groups):
                y = mat[0, i] * xs[0]
                for j in range(1, groups):
                    y = y + mat[j, i] * xs[j]
                place = i * BLK + at
                fwd_send[unit, place // quarter, pl.ds(pl.multiple_of(lax.rem(place, quarter), step), step), :] = y.astype(BF16)

        for k, other in others:
            forward_copy(unit, k, other).start()
        fwd_recv[unit, me] = fwd_send[unit, me]

    for chunk in range(chunks):
        loads[4 * chunk].wait()
        loads[4 * chunk + 1].wait()
        cut = lanes(chunk)
        for j in range(groups):
            at = slice(j * BLK, (j + 1) * BLK)
            gt_all[at, cut] = (cotangent[at, cut].astype(F32) * query[at, cut].astype(F32)).astype(BF16)
        forward(chunk, chunk, gt_all)

    ring.wait_recv()
    here = ids[...]
    tall = here.shape[0]
    above = jnp.concatenate([ends_recv[tall - 1:, LANES - 1:], here[:tall - 1, LANES - 1:]], axis=0)
    before = jnp.concatenate([above, here[:, :LANES - 1]], axis=1)
    start = (lax.broadcasted_iota(jnp.int32, here.shape, 0) == 0) & (lax.broadcasted_iota(jnp.int32, here.shape, 1) == 0)
    keep = jnp.where((here == before) & ((me > 0) | jnp.logical_not(start)), 1.0, 0.0)
    wide = BLK // LANES
    keep = jnp.concatenate(
        [jnp.concatenate([keep[j * wide + n:j * wide + n + 1] for n in range(wide)], axis=1) for j in range(groups)], axis=0,
    )
    keep_t[...] = keep.T
    if peers:
        for k, source in sources:
            small(0, k, source).wait_recv()
        for k, peer in peers:
            share_copy(k, peer).start()
    for chunk in range(chunks):
        loads[4 * chunk + 2].wait()
        loads[4 * chunk + 3].wait()
        cut = lanes(chunk)
        for j in range(groups):
            at = slice(j * BLK, (j + 1) * BLK)
            u_all[at, cut] = (keyed[at, cut].astype(F32) * values[at, cut].astype(F32) * keep_t[:, j:j + 1]).astype(BF16)
        forward(chunks + chunk, chunk, u_all)

    for kind in (2, 1):
        for k, source in sources:
            small(kind, k, source).wait_recv()
    if peers:
        for k, peer in peers:
            rest = pl.ds(pl.multiple_of(lax.rem(spot + crew - k, crew) * part, part), part)
            remote(
                pos_recv.at[:, rest], pos_recv.at[:, rest], share_send_sem.at[k], share_recv_sem.at[k], peer, "chan",
            ).wait_recv()
    else:
        for k, source in sources:
            small(0, k, source).wait_recv()
    for p in range(count):
        weight_all[p * share:(p + 1) * share, :] = weight_recv[p]
    whole = weight_all[...].astype(BF16)
    for p in range(count):
        filt[p] = lax.dot_general(pos_recv[p], whole, (((0,), (0,)), ((), ())), preferred_element_type=F32)
        coef_t[p] = coef_recv[p].T

    def rounded(x):
        return x.astype(BF16).astype(F32)

    def middle(unit, chunk, gated):
        for k, source in sources:
            forward_copy(unit, k, source).wait_recv()

        @pl.loop(0, quarter // step)
        def _(r):
            at = pl.ds(pl.multiple_of(r * step, step), step)
            xs = [fwd_recv[unit, p, at, :].astype(F32) for p in range(count)]
            cols = [coef_t[p, at, :] for p in range(count)]

            def own(k, p):
                return cols[p][:, k:k + 1]

            def cross(k, p):
                return cols[p][:, sections + k:sections + k + 1]

            for k in range(sections):
                xs = [rounded(own(k, p) * xs[p] + cross(k, p) * xs[p ^ (1 << k)]) for p in range(count)]
            for p in range(count):
                if gated:
                    dw_keep[chunk, p, at, :] = xs[p].astype(BF16)
                else:
                    dfilt[p, at, :] = (dw_keep[chunk, p, at, :].astype(F32) * xs[p]).astype(BF16)
            xs = [rounded(xs[p] * filt[p, at, lanes(chunk)]) for p in range(count)]
            for k in reversed(range(sections)):
                xs = [
                    rounded(own(k, p) * xs[p] + cross(k, p ^ (1 << k)) * xs[p ^ (1 << k)])
                    for p in range(count)
                ]
            for p in range(count):
                back_send[unit, p, at, :] = xs[p].astype(BF16)

        for k, other in others:
            back_copy(unit, k, other).start()
        back_recv[unit, me] = back_send[unit, me]
        if not gated:
            total = jnp.dot(pos_recv[0], dfilt[0], preferred_element_type=F32)
            for p in range(1, count):
                total = total + jnp.dot(pos_recv[p], dfilt[p], preferred_element_type=F32)
            total = total * scale
            for p in range(count):
                part_send[p, :, lanes(chunk)] = total[p * share:(p + 1) * share]

    for chunk in range(chunks):
        middle(chunk, chunk, True)
    for chunk in range(chunks):
        middle(chunks + chunk, chunk, False)
    for k, other in others:
        small(3, k, other).start()
    part_recv[me] = part_send[me]

    def final(unit, chunk, gated):
        for k, source in sources:
            back_copy(unit, k, source).wait_recv()

        @pl.loop(0, BLK // step)
        def _(r):
            at = pl.multiple_of(r * step, step)
            xs = []
            for i in range(groups):
                place = i * BLK + at
                xs.append(back_recv[unit, place // quarter, pl.ds(pl.multiple_of(lax.rem(place, quarter), step), step), :].astype(F32))
            for j in range(groups):
                y = mat[j, 0] * xs[0]
                for i in range(1, groups):
                    y = y + mat[j, i] * xs[i]
                half[j, pl.ds(at, step), :] = y.astype(BF16)

        cut = lanes(chunk)
        skip = gain[0:1, cut]
        for j in range(groups):
            at = slice(j * BLK, (j + 1) * BLK)
            y = rounded(jnp.dot(first[...], half[j], preferred_element_type=F32))
            if gated:
                du = (y + skip * gt_all[at, cut].astype(F32)) * keep_t[:, j:j + 1]
                grad_keyed[at, cut] = (du * values[at, cut].astype(F32)).astype(BF16)
                grad_values[at, cut] = (du * keyed[at, cut].astype(F32)).astype(BF16)
            else:
                total = y + skip * u_all[at, cut].astype(F32)
                mixed[at, cut] = (query[at, cut].astype(F32) * total).astype(BF16)
                grad_query[at, cut] = (cotangent[at, cut].astype(F32) * total).astype(BF16)

    stores = []

    def store(unit, chunk, pairs):
        cut = pl.ds(chunk * LANES, LANES)
        for n, (near, far) in enumerate(pairs):
            copy = pltpu.make_async_copy(near.at[:, cut], far.at[:, cut], store_sem.at[unit, n])
            copy.start()
            stores.append(copy)

    after = ((grad_keyed, keyed_out), (grad_values, values_out))
    ahead = ((mixed, mixed_out), (grad_query, query_out))
    for chunk in range(chunks):
        final(chunk, chunk, True)
        store(chunk, chunk, after)
    for chunk in range(chunks - 1):
        final(chunks + chunk, chunk, False)
        store(chunks + chunk, chunk, ahead)
    for k, source in sources:
        small(3, k, source).wait_recv()
    total = part_recv[0]
    for p in range(1, count):
        total = total + part_recv[p]
    grad_filter[...] = total
    final(2 * chunks - 1, chunks - 1, False)
    store(2 * chunks - 1, chunks - 1, ahead)
    for copy in stores:
        copy.wait()

    for k, peer in peers:
        share_copy(k, peer).wait_send()
    ring.wait_send()
    for k, other in others:
        for kind in range(4):
            small(kind, k, other).wait_send()
        for unit in range(2 * chunks):
            forward_copy(unit, k, other).wait_send()
            back_copy(unit, k, other).wait_send()


def on_device(
    query, keyed, values, cotangent, segment_ids, positions, filter_weight, skip_gain,
    first_factor, second_factor, self_coef, cross_coef,
):
    count = lax.axis_size("seq")
    sections = self_coef.shape[0]
    rows, width = query.shape
    groups = rows // BLK
    quarter = rows // count
    feats = positions.shape[1]
    share = filter_weight.shape[0]
    chunks = width // LANES
    units = 2 * chunks
    kinds = -(-2 * sections // 8) * 8
    scale = 1.0 / math.sqrt(rows * count)
    vmem = pl.BlockSpec(memory_space=pltpu.VMEM)
    field = jax.ShapeDtypeStruct((rows, width), BF16)
    crew = lax.axis_size("chan")
    tall = rows // LANES
    return pl.pallas_call(
        functools.partial(kernel, count, sections, scale),
        out_shape=(field, field, field, field, jax.ShapeDtypeStruct((share, width), F32)),
        in_specs=[pl.BlockSpec(memory_space=pltpu.HBM)] * 12,
        out_specs=(pl.BlockSpec(memory_space=pltpu.HBM),) * 4 + (vmem,),
        scratch_shapes=[
            pltpu.VMEM((rows, width), BF16),
            pltpu.VMEM((rows, width), BF16),
            pltpu.VMEM((rows, width), BF16),
            pltpu.VMEM((rows, width), BF16),
            pltpu.VMEM((tall, LANES), jnp.int32),
            pltpu.VMEM((feats, rows), BF16),
            pltpu.VMEM((share, width), BF16),
            pltpu.VMEM((1, width), F32),
            pltpu.VMEM((BLK, BLK), BF16),
            pltpu.VMEM(second_factor.shape, BF16),
            pltpu.VMEM((sections, rows), BF16),
            pltpu.VMEM((sections, rows), BF16),
            pltpu.VMEM((groups, groups, min(16, quarter), LANES), F32),
            pltpu.VMEM((count, share, width), F32),
            pltpu.VMEM((rows, width), BF16),
            pltpu.VMEM((rows, width), BF16),
            pltpu.VMEM((rows, width), BF16),
            pltpu.VMEM((rows, width), BF16),
            pltpu.VMEM((BLK, BLK), BF16),
            pltpu.VMEM((BLK, groups), F32),
            pltpu.VMEM((rows, width), BF16),
            pltpu.VMEM((rows, width), BF16),
            pltpu.VMEM((groups, BLK, LANES), BF16),
            pltpu.VMEM((units, count, quarter, LANES), BF16),
            pltpu.VMEM((units, count, quarter, LANES), BF16),
            pltpu.VMEM((units, count, quarter, LANES), BF16),
            pltpu.VMEM((units, count, quarter, LANES), BF16),
            pltpu.VMEM((count, feats, quarter), BF16),
            pltpu.VMEM((count, feats, quarter), BF16),
            pltpu.VMEM((share, width), F32),
            pltpu.VMEM((count, share, width), F32),
            pltpu.VMEM((tall, LANES), jnp.int32),
            pltpu.VMEM((count, kinds, quarter), F32),
            pltpu.VMEM((count, quarter, kinds), F32),
            pltpu.VMEM((count, kinds, quarter), F32),
            pltpu.VMEM((feats, width), F32),
            pltpu.VMEM((count, quarter, width), F32),
            pltpu.VMEM((chunks, count, quarter, LANES), BF16),
            pltpu.VMEM((count, quarter, LANES), BF16),
            pltpu.VMEM((count, share, width), F32),
            pltpu.SemaphoreType.DMA((2, units, count)),
            pltpu.SemaphoreType.DMA((2, units, count)),
            pltpu.SemaphoreType.DMA((4, count)),
            pltpu.SemaphoreType.DMA((4, count)),
            pltpu.SemaphoreType.DMA((2,)),
            pltpu.SemaphoreType.DMA((chunks, 4)),
            pltpu.SemaphoreType.DMA((8,)),
            pltpu.SemaphoreType.DMA((crew,)),
            pltpu.SemaphoreType.DMA((crew,)),
            pltpu.SemaphoreType.DMA((units, 2)),
        ],
        compiler_params=pltpu.CompilerParams(
            collective_id=0, has_side_effects=True, vmem_limit_bytes=58 * 1024 * 1024
        ),
        cost_estimate=pl.CostEstimate(flops=2 * 10**9, bytes_accessed=8 * rows * width * 2, transcendentals=0),
    )(
        query, keyed, values, cotangent, segment_ids.reshape(tall, LANES), positions.T, filter_weight,
        skip_gain[None, :], first_factor, second_factor, self_coef[:, 0], cross_coef[:, 0],
    )


def solution(mesh):
    field = P(("groups", "seq"), "chan")
    return jax.shard_map(
        on_device,
        mesh=mesh,
        in_specs=(
            field, field, field, field, P(("groups", "seq")), P(("groups", "seq"), None),
            P("seq", "chan"), P("chan"), P(), P(), P(None, "seq", None), P(None, "seq", None),
        ),
        out_specs=(field,) * 5,
        check_vma=False,
    )
```

```python
import functools
import math

import jax
import jax.numpy as jnp
from jax import lax
from jax.experimental import pallas as pl
from jax.experimental.pallas import tpu as pltpu
from jax.sharding import PartitionSpec as P

BLK = 256
LANES = 128
F32 = jnp.float32
BF16 = jnp.bfloat16


def kernel(
    count, sections, scale,
    query_in, keyed_in, values_in, cotangent_in, ids_in, pos_in, weight_in, gain_in, first_in, second_in,
    self_in, cross_in,
    mixed_out, query_out, keyed_out, values_out, grad_filter,
    mixed, grad_query, grad_keyed, grad_values, ids, pos, weight, gain, first, second, self_coef, cross_coef, mat, part_recv,
    query, keyed, values, cotangent, first_t, keep_t, u_all, gt_all, half, fwd_send, fwd_recv, back_send, back_recv,
    pos_send, pos_recv, weight_send, weight_recv, ends_recv, coef_recv, coef_t,
    coef_send, weight_all, filt, dw_keep, dfilt, part_send,
    field_send_sem, field_recv_sem, small_send_sem, small_recv_sem, ends_sem, load_sem, tiny_sem, share_send_sem, share_recv_sem, store_sem,
):
    rows, width = query.shape
    groups = rows // BLK
    quarter = rows // count
    share = weight.shape[0]
    chunks = width // LANES
    me = lax.axis_index("seq")
    others = [(k, lax.rem(me + k, count)) for k in range(1, count)]
    sources = [(k, lax.rem(me + count - k, count)) for k in range(1, count)]
    feats = pos_in.shape[0]
    crew = lax.axis_size("chan")
    split = crew if (feats // crew) % 16 == 0 else 1
    part = feats // split
    spot = lax.axis_index("chan")
    if split > 1:
        mine = pl.ds(pl.multiple_of(spot * part, part), part)
        peers = [(k, lax.rem(spot + k, crew)) for k in range(1, crew)]
    else:
        mine, peers = slice(None), []

    barrier = pltpu.get_barrier_semaphore()
    for _, other in others:
        pl.semaphore_signal(barrier, inc=1, device_id={"seq": other}, device_id_type=pl.DeviceIdType.MESH)
    for _, peer in peers:
        pl.semaphore_signal(barrier, inc=1, device_id={"chan": peer}, device_id_type=pl.DeviceIdType.MESH)

    def remote(src, dst, send, recv, other, axis="seq"):
        return pltpu.make_async_remote_copy(
            src_ref=src, dst_ref=dst, send_sem=send, recv_sem=recv,
            device_id={axis: other}, device_id_type=pl.DeviceIdType.MESH,
        )

    loads = []
    for chunk in range(chunks):
        cut = pl.ds(chunk * LANES, LANES)
        for n, (far, near) in enumerate(((query_in, query), (cotangent_in, cotangent), (keyed_in, keyed), (values_in, values))):
            loads.append(pltpu.make_async_copy(far.at[:, cut], near.at[:, cut], load_sem.at[chunk, n]))
    order = [4 * chunk + n for n0 in (0, 2) for chunk in range(chunks) for n in (n0, n0 + 1)]
    tiny = [
        pltpu.make_async_copy(far, near, tiny_sem.at[n])
        for n, (far, near) in enumerate((
            (pos_in, pos), (self_in, self_coef), (cross_in, cross_coef), (weight_in, weight), (ids_in, ids),
            (first_in, first), (second_in, second), (gain_in, gain),
        ))
    ]
    for copy in tiny:
        copy.start()
    for at in order:
        loads[at].start()
    for copy in tiny:
        copy.wait()

    coef_send[...] = jnp.zeros_like(coef_send)
    for p in range(count):
        cut = slice(p * quarter, (p + 1) * quarter)
        pos_send[p] = pos[:, cut]
        coef_send[p, :sections, :] = self_coef[:, cut].astype(F32)
        coef_send[p, sections:2 * sections, :] = cross_coef[:, cut].astype(F32)
    weight_send[...] = weight[...].astype(F32)

    pl.semaphore_wait(barrier, count - 1 + len(peers))

    def small(kind, k, other):
        send, recv = small_send_sem.at[kind, k], small_recv_sem.at[kind, k]
        if kind == 0:
            return remote(pos_send.at[other, mine], pos_recv.at[me, mine], send, recv, other)
        if kind == 1:
            return remote(weight_send, weight_recv.at[me], send, recv, other)
        if kind == 2:
            return remote(coef_send.at[other], coef_recv.at[me], send, recv, other)
        return remote(part_send.at[other], part_recv.at[me], send, recv, other)

    ring = remote(ids, ends_recv, ends_sem.at[0], ends_sem.at[1], lax.rem(me + 1, count))
    ring.start()
    for kind in (2, 1, 0):
        for k, other in others:
            small(kind, k, other).start()
    pos_recv[me, mine] = pos_send[me, mine]
    weight_recv[me] = weight_send[...]
    coef_recv[me] = coef_send[me]

    def share_copy(k, peer):
        return remote(
            pos_recv.at[:, mine], pos_recv.at[:, mine], share_send_sem.at[k], share_recv_sem.at[k], peer, "chan",
        )

    def forward_copy(unit, k, other):
        return remote(
            fwd_send.at[unit, other], fwd_recv.at[unit, me],
            field_send_sem.at[0, unit, k], field_recv_sem.at[0, unit, k], other,
        )

    def back_copy(unit, k, other):
        return remote(
            back_send.at[unit, other], back_recv.at[unit, me],
            field_send_sem.at[1, unit, k], field_recv_sem.at[1, unit, k], other,
        )

    def lanes(chunk):
        return slice(chunk * LANES, (chunk + 1) * LANES)

    step = min(16, quarter)
    first_t[...] = first[...].astype(F32).T.astype(BF16)
    table = second[...].astype(F32)
    for j in range(groups):
        for i in range(groups):
            mat[j, i] = jnp.broadcast_to(table[j:j + 1, i:i + 1], mat.shape[2:])

    def forward(unit, chunk, source):
        for j in range(groups):
            x = source[j * BLK:(j + 1) * BLK, lanes(chunk)]
            half[j] = jnp.dot(first_t[...], x, preferred_element_type=F32).astype(BF16)

        if quarter % BLK == 0:
            per = quarter // BLK
            for k, other in others + [(0, me)]:
                mats = [[mat[j, other * per + i] for i in range(per)] for j in range(groups)]

                @pl.loop(0, BLK // step)
                def _(r, mats=mats, k=k, other=other):
                    at = pl.multiple_of(r * step, step)
                    xs = [half[j, pl.ds(at, step), :].astype(F32) for j in range(groups)]
                    for i in range(per):
                        y = mats[0][i] * xs[0]
                        for j in range(1, groups):
                            y = y + mats[j][i] * xs[j]
                        place = pl.ds(pl.multiple_of(i * BLK + at, step), step)
                        if k == 0:
                            fwd_recv[unit, me, place, :] = y.astype(BF16)
                        else:
                            fwd_send[unit, other, place, :] = y.astype(BF16)

                if k:
                    forward_copy(unit, k, other).start()
            return

        @pl.loop(0, BLK // step)
        def _(r):
            at = pl.multiple_of(r * step, step)
            xs = [half[j, pl.ds(at, step), :].astype(F32) for j in range(groups)]
            for i in range(groups):
                y = mat[0, i] * xs[0]
                for j in range(1, groups):
                    y = y + mat[j, i] * xs[j]
                place = i * BLK + at
                fwd_send[unit, place // quarter, pl.ds(pl.multiple_of(lax.rem(place, quarter), step), step), :] = y.astype(BF16)

        for k, other in others:
            forward_copy(unit, k, other).start()
        fwd_recv[unit, me] = fwd_send[unit, me]

    for chunk in range(chunks):
        loads[4 * chunk].wait()
        loads[4 * chunk + 1].wait()
        cut = lanes(chunk)
        for j in range(groups):
            at = slice(j * BLK, (j + 1) * BLK)
            gt_all[at, cut] = (cotangent[at, cut].astype(F32) * query[at, cut].astype(F32)).astype(BF16)
        forward(chunk, chunk, gt_all)

    ring.wait_recv()
    here = ids[...]
    tall = here.shape[0]
    above = jnp.concatenate([ends_recv[tall - 1:, LANES - 1:], here[:tall - 1, LANES - 1:]], axis=0)
    before = jnp.concatenate([above, here[:, :LANES - 1]], axis=1)
    start = (lax.broadcasted_iota(jnp.int32, here.shape, 0) == 0) & (lax.broadcasted_iota(jnp.int32, here.shape, 1) == 0)
    keep = jnp.where((here == before) & ((me > 0) | jnp.logical_not(start)), 1.0, 0.0)
    wide = BLK // LANES
    keep = jnp.concatenate(
        [jnp.concatenate([keep[j * wide + n:j * wide + n + 1] for n in range(wide)], axis=1) for j in range(groups)], axis=0,
    )
    keep_t[...] = keep.T
    if peers:
        for k, source in sources:
            small(0, k, source).wait_recv()
        for k, peer in peers:
            share_copy(k, peer).start()
    for chunk in range(chunks):
        loads[4 * chunk + 2].wait()
        loads[4 * chunk + 3].wait()
        cut = lanes(chunk)
        for j in range(groups):
            at = slice(j * BLK, (j + 1) * BLK)
            u_all[at, cut] = (keyed[at, cut].astype(F32) * values[at, cut].astype(F32) * keep_t[:, j:j + 1]).astype(BF16)
        forward(chunks + chunk, chunk, u_all)

    for kind in (2, 1):
        for k, source in sources:
            small(kind, k, source).wait_recv()
    if peers:
        for k, peer in peers:
            rest = pl.ds(pl.multiple_of(lax.rem(spot + crew - k, crew) * part, part), part)
            remote(
                pos_recv.at[:, rest], pos_recv.at[:, rest], share_send_sem.at[k], share_recv_sem.at[k], peer, "chan",
            ).wait_recv()
    else:
        for k, source in sources:
            small(0, k, source).wait_recv()
    for p in range(count):
        weight_all[p * share:(p + 1) * share, :] = weight_recv[p]
    whole = weight_all[...].astype(BF16)
    for p in range(count):
        filt[p] = lax.dot_general(pos_recv[p], whole, (((0,), (0,)), ((), ())), preferred_element_type=F32)
        coef_t[p] = coef_recv[p].T

    def rounded(x):
        return x.astype(BF16).astype(F32)

    def middle(unit, chunk, gated):
        for k, source in sources:
            forward_copy(unit, k, source).wait_recv()

        @pl.loop(0, quarter // step)
        def _(r):
            at = pl.ds(pl.multiple_of(r * step, step), step)
            xs = [fwd_recv[unit, p, at, :].astype(F32) for p in range(count)]
            cols = [coef_t[p, at, :] for p in range(count)]

            def own(k, p):
                return cols[p][:, k:k + 1]

            def cross(k, p):
                return cols[p][:, sections + k:sections + k + 1]

            for k in range(sections):
                xs = [rounded(own(k, p) * xs[p] + cross(k, p) * xs[p ^ (1 << k)]) for p in range(count)]
            for p in range(count):
                if gated:
                    dw_keep[chunk, p, at, :] = xs[p].astype(BF16)
                else:
                    dfilt[p, at, :] = (dw_keep[chunk, p, at, :].astype(F32) * xs[p]).astype(BF16)
            xs = [rounded(xs[p] * filt[p, at, lanes(chunk)]) for p in range(count)]
            for k in reversed(range(sections)):
                xs = [
                    rounded(own(k, p) * xs[p] + cross(k, p ^ (1 << k)) * xs[p ^ (1 << k)])
                    for p in range(count)
                ]
            for p in range(count):
                back_send[unit, p, at, :] = xs[p].astype(BF16)

        for k, other in others:
            back_copy(unit, k, other).start()
        back_recv[unit, me] = back_send[unit, me]
        if not gated:
            total = jnp.dot(pos_recv[0], dfilt[0], preferred_element_type=F32)
            for p in range(1, count):
                total = total + jnp.dot(pos_recv[p], dfilt[p], preferred_element_type=F32)
            total = total * scale
            for p in range(count):
                part_send[p, :, lanes(chunk)] = total[p * share:(p + 1) * share]

    for chunk in range(chunks):
        middle(chunk, chunk, True)
    for chunk in range(chunks):
        middle(chunks + chunk, chunk, False)
    for k, other in others:
        small(3, k, other).start()
    part_recv[me] = part_send[me]

    def final(unit, chunk, gated):
        for k, source in sources:
            back_copy(unit, k, source).wait_recv()

        @pl.loop(0, BLK // step)
        def _(r):
            at = pl.multiple_of(r * step, step)
            xs = []
            for i in range(groups):
                place = i * BLK + at
                xs.append(back_recv[unit, place // quarter, pl.ds(pl.multiple_of(lax.rem(place, quarter), step), step), :].astype(F32))
            for j in range(groups):
                y = mat[j, 0] * xs[0]
                for i in range(1, groups):
                    y = y + mat[j, i] * xs[i]
                half[j, pl.ds(at, step), :] = y.astype(BF16)

        cut = lanes(chunk)
        skip = gain[0:1, cut]
        for j in range(groups):
            at = slice(j * BLK, (j + 1) * BLK)
            y = rounded(jnp.dot(first[...], half[j], preferred_element_type=F32))
            if gated:
                du = (y + skip * gt_all[at, cut].astype(F32)) * keep_t[:, j:j + 1]
                grad_keyed[at, cut] = (du * values[at, cut].astype(F32)).astype(BF16)
                grad_values[at, cut] = (du * keyed[at, cut].astype(F32)).astype(BF16)
            else:
                total = y + skip * u_all[at, cut].astype(F32)
                mixed[at, cut] = (query[at, cut].astype(F32) * total).astype(BF16)
                grad_query[at, cut] = (cotangent[at, cut].astype(F32) * total).astype(BF16)

    stores = []

    def store(unit, chunk, pairs):
        cut = pl.ds(chunk * LANES, LANES)
        for n, (near, far) in enumerate(pairs):
            copy = pltpu.make_async_copy(near.at[:, cut], far.at[:, cut], store_sem.at[unit, n])
            copy.start()
            stores.append(copy)

    after = ((grad_keyed, keyed_out), (grad_values, values_out))
    ahead = ((mixed, mixed_out), (grad_query, query_out))
    for chunk in range(chunks):
        final(chunk, chunk, True)
        store(chunk, chunk, after)
    for chunk in range(chunks - 1):
        final(chunks + chunk, chunk, False)
        store(chunks + chunk, chunk, ahead)
    for k, source in sources:
        small(3, k, source).wait_recv()
    total = part_recv[0]
    for p in range(1, count):
        total = total + part_recv[p]
    grad_filter[...] = total
    final(2 * chunks - 1, chunks - 1, False)
    store(2 * chunks - 1, chunks - 1, ahead)
    for copy in stores:
        copy.wait()

    for k, peer in peers:
        share_copy(k, peer).wait_send()
    ring.wait_send()
    for k, other in others:
        for kind in range(4):
            small(kind, k, other).wait_send()
        for unit in range(2 * chunks):
            forward_copy(unit, k, other).wait_send()
            back_copy(unit, k, other).wait_send()


def on_device(
    query, keyed, values, cotangent, segment_ids, positions, filter_weight, skip_gain,
    first_factor, second_factor, self_coef, cross_coef,
):
    count = lax.axis_size("seq")
    sections = self_coef.shape[0]
    rows, width = query.shape
    groups = rows // BLK
    quarter = rows // count
    feats = positions.shape[1]
    share = filter_weight.shape[0]
    chunks = width // LANES
    units = 2 * chunks
    kinds = -(-2 * sections // 8) * 8
    scale = 1.0 / math.sqrt(rows * count)
    vmem = pl.BlockSpec(memory_space=pltpu.VMEM)
    field = jax.ShapeDtypeStruct((rows, width), BF16)
    crew = lax.axis_size("chan")
    tall = rows // LANES
    return pl.pallas_call(
        functools.partial(kernel, count, sections, scale),
        out_shape=(field, field, field, field, jax.ShapeDtypeStruct((share, width), F32)),
        in_specs=[pl.BlockSpec(memory_space=pltpu.HBM)] * 12,
        out_specs=(pl.BlockSpec(memory_space=pltpu.HBM),) * 4 + (vmem,),
        scratch_shapes=[
            pltpu.VMEM((rows, width), BF16),
            pltpu.VMEM((rows, width), BF16),
            pltpu.VMEM((rows, width), BF16),
            pltpu.VMEM((rows, width), BF16),
            pltpu.VMEM((tall, LANES), jnp.int32),
            pltpu.VMEM((feats, rows), BF16),
            pltpu.VMEM((share, width), BF16),
            pltpu.VMEM((1, width), F32),
            pltpu.VMEM((BLK, BLK), BF16),
            pltpu.VMEM(second_factor.shape, BF16),
            pltpu.VMEM((sections, rows), BF16),
            pltpu.VMEM((sections, rows), BF16),
            pltpu.VMEM((groups, groups, min(16, quarter), LANES), F32),
            pltpu.VMEM((count, share, width), F32),
            pltpu.VMEM((rows, width), BF16),
            pltpu.VMEM((rows, width), BF16),
            pltpu.VMEM((rows, width), BF16),
            pltpu.VMEM((rows, width), BF16),
            pltpu.VMEM((BLK, BLK), BF16),
            pltpu.VMEM((BLK, groups), F32),
            pltpu.VMEM((rows, width), BF16),
            pltpu.VMEM((rows, width), BF16),
            pltpu.VMEM((groups, BLK, LANES), BF16),
            pltpu.VMEM((units, count, quarter, LANES), BF16),
            pltpu.VMEM((units, count, quarter, LANES), BF16),
            pltpu.VMEM((units, count, quarter, LANES), BF16),
            pltpu.VMEM((units, count, quarter, LANES), BF16),
            pltpu.VMEM((count, feats, quarter), BF16),
            pltpu.VMEM((count, feats, quarter), BF16),
            pltpu.VMEM((share, width), F32),
            pltpu.VMEM((count, share, width), F32),
            pltpu.VMEM((tall, LANES), jnp.int32),
            pltpu.VMEM((count, kinds, quarter), F32),
            pltpu.VMEM((count, quarter, kinds), F32),
            pltpu.VMEM((count, kinds, quarter), F32),
            pltpu.VMEM((feats, width), F32),
            pltpu.VMEM((count, quarter, width), F32),
            pltpu.VMEM((chunks, count, quarter, LANES), BF16),
            pltpu.VMEM((count, quarter, LANES), BF16),
            pltpu.VMEM((count, share, width), F32),
            pltpu.SemaphoreType.DMA((2, units, count)),
            pltpu.SemaphoreType.DMA((2, units, count)),
            pltpu.SemaphoreType.DMA((4, count)),
            pltpu.SemaphoreType.DMA((4, count)),
            pltpu.SemaphoreType.DMA((2,)),
            pltpu.SemaphoreType.DMA((chunks, 4)),
            pltpu.SemaphoreType.DMA((8,)),
            pltpu.SemaphoreType.DMA((crew,)),
            pltpu.SemaphoreType.DMA((crew,)),
            pltpu.SemaphoreType.DMA((units, 2)),
        ],
        compiler_params=pltpu.CompilerParams(
            collective_id=0, has_side_effects=True, vmem_limit_bytes=49 * 1024 * 1024
        ),
        cost_estimate=pl.CostEstimate(flops=2 * 10**9, bytes_accessed=8 * rows * width * 2, transcendentals=0),
    )(
        query, keyed, values, cotangent, segment_ids.reshape(tall, LANES), positions.T, filter_weight,
        skip_gain[None, :], first_factor, second_factor, self_coef[:, 0], cross_coef[:, 0],
    )


def solution(mesh):
    field = P(("groups", "seq"), "chan")
    return jax.shard_map(
        on_device,
        mesh=mesh,
        in_specs=(
            field, field, field, field, P(("groups", "seq")), P(("groups", "seq"), None),
            P("seq", "chan"), P("chan"), P(), P(), P(None, "seq", None), P(None, "seq", None),
        ),
        out_specs=(field,) * 5,
        check_vma=False,
    )
```
